512 devices in a mesh: section: 8 (over x_hi, y), tp: 64 (over x_lo, z, core).
Axes of the slice: x: 4 (x_hi: 2, x_lo: 2; x = x_hi * 2 + x_lo), y: 4, z: 16, core: 2. Of those that a mesh axis runs over, the one named last changes fastest.
Arguments:
- resid: bfloat16 [8, 16, 8192], P('section', None, 'tp'), may hold values from -6 to 6
- norm_gain: bfloat16 [8, 8192], P('section'), may hold values from 0.5 to 1.5
- query_weight: bfloat16 [8, 8192, 8192], P('section', None, 'tp'), may hold values from -0.0625 to 0.0625
- key_value_weight: bfloat16 [8, 8192, 2048], P('section', None, 'tp'), may hold values from -0.0625 to 0.0625
- out_weight: bfloat16 [8, 8192, 8192], P('section', None, 'tp'), may hold values from -0.25 to 0.25
- key_value_cache: bfloat16 [8, 16, 384, 2048], P('section', None, 'tp'), may hold values from -51 to 51
- lengths: int32 [8, 16], P('section'), may hold values from 1 to 384, as said below
- positions: int32 [8, 16], P('section'), may hold values from 1 to 8575, as said below
Outputs:
- next_input: bfloat16 [8, 16, 8192], P('section', None, 'tp')
The draws below stay inside these ranges and needn't reach their ends.
Inputs may be any that keep to these rules, and one draw needn't show every extreme that they name: `lengths`: at most 384; in every section some row has exactly 384. `positions`: each row's position is at least its length and at most its length + 8191; in every section some row has exactly 8575.
All inputs are finite; a program needn't handle non-finite values.
Results may differ from the reference program's by a relative error of at most 0.012.
The reference program's roundings to bfloat16 on the way count: a program that leaves them out, or rounds other values in their place, can miss the bound.
Values may be sent and summed in bfloat16 or wider, within the bound.
No kernel may reach another device: no remote copies, remote signals or barrier semaphores. Data moves between devices by JAX's collectives and lax.ppermute only.
A program may use at most 192 MiB of HBM per device.

```python
import math
import jax
import jax.numpy as jnp
from jax import lax

MODEL_WIDTH = 8192
HEAD_WIDTH = 128
KEY_VALUE_HEADS = 8
MICRO_ROWS = 16
SECTION_COUNT = 8
QUERY_HEADS = 64
CONTEXT_SLOTS = 384


def shared_lengths(key):
    base_len = jax.random.randint(key, (SECTION_COUNT, MICRO_ROWS), 1, CONTEXT_SLOTS + 1, dtype=jnp.int32)
    full_row = jax.random.randint(jax.random.fold_in(key, 5), (SECTION_COUNT, 1), 0, MICRO_ROWS, dtype=jnp.int32)
    row_index = jnp.arange(MICRO_ROWS, dtype=jnp.int32)[None, :]
    return jnp.where(row_index == full_row, CONTEXT_SLOTS, base_len).astype(jnp.int32)


def draw_lengths(key, part):
    return shared_lengths(key)


def draw_positions(key, part):
    base_len = shared_lengths(key)
    key = jax.random.fold_in(key, 23)
    offsets = jax.random.randint(key, (SECTION_COUNT, MICRO_ROWS), 0, 8192, dtype=jnp.int32)
    offsets = jnp.where(base_len == CONTEXT_SLOTS, 8191, offsets).astype(jnp.int32)
    return (base_len + offsets).astype(jnp.int32)


def draw_key_value_cache(key, part):
    key = jax.random.fold_in(key, 11)
    first_key = jax.random.fold_in(key, 0)
    array_shape = (SECTION_COUNT, MICRO_ROWS, CONTEXT_SLOTS, 2 * KEY_VALUE_HEADS * HEAD_WIDTH)
    values = jnp.clip(jax.random.normal(first_key, array_shape, jnp.float32), -6.0, 6.0)
    return values.astype(jnp.bfloat16)


def steps_of(key, extent, cuts, smallest, top_value):
    level, own = 1.0, jax.random.fold_in(key, 6)
    for axis_at, parts in cuts:
        steps = jnp.exp(jax.random.uniform(jax.random.fold_in(own, axis_at), (parts,), jnp.float32, smallest / len(cuts), top_value / len(cuts)))
        level = level * jnp.repeat(steps, extent[axis_at] // parts).reshape([-1 if axis == axis_at else 1 for axis in range(len(extent))])
    return level


def gaussian(own_key, shape, deviation, bound, pieces=(), kind=jnp.bfloat16):
    loudness = steps_of(own_key, shape, pieces, -0.22, 0.18) if pieces else 1.0
    entries = jax.random.normal(own_key, shape, jnp.float32) * deviation * loudness
    return jnp.minimum(jnp.maximum(entries, -bound), bound).astype(kind)


def setup_inputs(seed: int = 0) -> dict:
    streams_of = jax.random.split(jax.random.key(seed), 9)
    resid = gaussian(streams_of[0], (SECTION_COUNT, MICRO_ROWS, MODEL_WIDTH), 1.0, 6.0, ((0, 8), (2, 64)))
    norm_gain = jnp.clip(1.0 + 0.1 * jax.random.normal(streams_of[1], (SECTION_COUNT, MODEL_WIDTH), jnp.float32), 0.5, 1.5).astype(jnp.bfloat16)
    query_weight = gaussian(streams_of[2], (SECTION_COUNT, MODEL_WIDTH, QUERY_HEADS * HEAD_WIDTH), MODEL_WIDTH ** -0.5, 0.0625, ((0, 8), (2, 64)))
    key_value_weight = gaussian(streams_of[3], (SECTION_COUNT, MODEL_WIDTH, 2 * KEY_VALUE_HEADS * HEAD_WIDTH), MODEL_WIDTH ** -0.5, 0.0625, ((0, 8), (2, 64)))
    out_weight = gaussian(streams_of[4], (SECTION_COUNT, QUERY_HEADS * HEAD_WIDTH, MODEL_WIDTH), (QUERY_HEADS * HEAD_WIDTH // 16) ** -0.5, 0.25, ((0, 8), (2, 64)))
    key_value_cache = draw_key_value_cache(jax.random.fold_in(streams_of[8], 71), 0)
    lengths = draw_lengths(jax.random.fold_in(streams_of[8], 71), 0)
    positions = draw_positions(jax.random.fold_in(streams_of[8], 71), 0)
    return {"resid": resid, "norm_gain": norm_gain, "query_weight": query_weight, "key_value_weight": key_value_weight, "out_weight": out_weight, "key_value_cache": key_value_cache, "lengths": lengths, "positions": positions}


def apply_rotary(vectors, token_positions):
    half_size = vectors.shape[-1] // 2
    freqs = jnp.exp(-math.log(500000.0) * 2.0 * jnp.arange(half_size, dtype=jnp.float32) / vectors.shape[-1])
    angles = token_positions.astype(jnp.float32)[:, None, None] * freqs
    cosine = jnp.cos(angles)
    sine = jnp.sin(angles)
    first = vectors[..., :half_size]
    second = vectors[..., half_size:]
    return jnp.concatenate([first * cosine - second * sine, second * cosine + first * sine], axis=-1)

def one_section(operands):
    resid, norm_gain, query_weight, key_value_weight, out_weight, key_value_cache, lengths, positions = operands
    widened = resid.astype(jnp.float32)
    meansq = lax.optimization_barrier(jnp.mean(widened * widened, axis=-1, keepdims=True))
    normed = (widened * lax.rsqrt(meansq + 1e-05) * norm_gain.astype(jnp.float32)).astype(jnp.bfloat16)
    query_rows = jnp.dot(normed, query_weight, preferred_element_type=jnp.float32).reshape(MICRO_ROWS, QUERY_HEADS, HEAD_WIDTH)
    query_rows = apply_rotary(query_rows, positions).astype(jnp.bfloat16)
    key_value_rows = jnp.dot(normed, key_value_weight, preferred_element_type=jnp.float32).astype(jnp.bfloat16)
    fresh_key = apply_rotary(key_value_rows[:, :KEY_VALUE_HEADS * HEAD_WIDTH].reshape(MICRO_ROWS, KEY_VALUE_HEADS, HEAD_WIDTH).astype(jnp.float32), positions).astype(jnp.bfloat16)
    fresh_value = key_value_rows[:, KEY_VALUE_HEADS * HEAD_WIDTH:].reshape(MICRO_ROWS, KEY_VALUE_HEADS, HEAD_WIDTH)
    stored_keys = key_value_cache[:, :, :KEY_VALUE_HEADS * HEAD_WIDTH].reshape(MICRO_ROWS, CONTEXT_SLOTS, KEY_VALUE_HEADS, HEAD_WIDTH).astype(jnp.float32)
    stored_values = key_value_cache[:, :, KEY_VALUE_HEADS * HEAD_WIDTH:].reshape(MICRO_ROWS, CONTEXT_SLOTS, KEY_VALUE_HEADS, HEAD_WIDTH).astype(jnp.float32)
    queries_per_group = QUERY_HEADS // KEY_VALUE_HEADS
    query_groups = query_rows.astype(jnp.float32).reshape(MICRO_ROWS, KEY_VALUE_HEADS, queries_per_group, HEAD_WIDTH)
    factor = 1.0 / math.sqrt(HEAD_WIDTH)
    scores = jnp.einsum('rkgd,rtkd->rkgt', query_groups, stored_keys) * factor
    live_mask = (jnp.arange(CONTEXT_SLOTS, dtype=jnp.int32)[None, :] < lengths[:, None])[:, None, None, :]
    new_score = jnp.einsum('rkgd,rkd->rkg', query_groups, fresh_key.astype(jnp.float32)) * factor
    peak_score = jnp.maximum(lax.optimization_barrier(jnp.max(jnp.where(live_mask, scores, -1e+30), axis=-1)), new_score)
    weights = jnp.where(live_mask, jnp.exp(scores - peak_score[..., None]), 0.0)
    new_weight = jnp.exp(new_score - peak_score)
    totals = lax.optimization_barrier(jnp.sum(weights, axis=-1)) + new_weight
    mixture = jnp.einsum('rkgt,rtkd->rkgd', weights, stored_values)
    mixture = mixture + new_weight[..., None] * fresh_value.astype(jnp.float32)[:, :, None, :]
    attn = (mixture / totals[..., None]).reshape(MICRO_ROWS, QUERY_HEADS * HEAD_WIDTH).astype(jnp.bfloat16)
    projected = jnp.dot(attn, out_weight, preferred_element_type=jnp.float32)
    return (widened + projected).astype(jnp.bfloat16)

def reference(resid, norm_gain, query_weight, key_value_weight, out_weight, key_value_cache, lengths, positions):
    updated = lax.map(one_section, (resid, norm_gain, query_weight, key_value_weight, out_weight, key_value_cache, lengths, positions))
    return jnp.roll(updated, 1, axis=0)
```

```python
import math

import jax
import jax.numpy as jnp
from jax import lax
from jax.sharding import Mesh
from jax.sharding import PartitionSpec as P

HEAD_WIDTH = 128
KEY_VALUE_HEADS = 8
MINOR = ("x", "z", "c")


def rotary_tables(token_positions):
    half_size = HEAD_WIDTH // 2
    freqs = jnp.exp(
        -math.log(500000.0) * 2.0 * jnp.arange(half_size, dtype=jnp.float32) / HEAD_WIDTH
    )
    angles = token_positions.astype(jnp.float32)[:, None] * freqs
    return jnp.cos(angles), jnp.sin(angles)


def rotate(vectors, cosine, sine):
    half_size = vectors.shape[-1] // 2
    first = vectors[..., :half_size]
    second = vectors[..., half_size:]
    return jnp.concatenate(
        [first * cosine - second * sine, second * cosine + first * sine], axis=-1
    )


def spread(part):
    line = lax.axis_size("z")
    copies = jnp.broadcast_to(part[None], (line,) + part.shape)
    along = lax.all_to_all(copies, "z", 0, 0)
    full = lax.all_gather(along, ("x", "c"))
    return full.reshape((lax.axis_size("x"), lax.axis_size("c"), line) + part.shape)


def body(
    resid,
    norm_gain,
    query_weight,
    key_value_weight,
    out_weight,
    key_value_cache,
    lengths,
    positions,
):
    rows = resid.shape[1]
    devices = lax.axis_size("x") * lax.axis_size("z") * lax.axis_size("c")
    groups = KEY_VALUE_HEADS
    members = devices // groups
    own_rows = rows // members
    me = lax.axis_index(MINOR)
    group, member = me // members, me % members
    span = key_value_cache.shape[2]

    pieces = key_value_cache[0].reshape(members, own_rows, span, 2, groups, HEAD_WIDTH)
    pieces = pieces.transpose(4, 0, 3, 2, 1, 5).reshape(
        devices, 2 * span * own_rows, HEAD_WIDTH
    )
    stored = lax.all_to_all(pieces, MINOR, 0, 0)

    gathered = spread(resid[0])
    widened = gathered.transpose(3, 0, 2, 1, 4).reshape(rows, -1).astype(jnp.float32)
    meansq = jnp.mean(widened * widened, axis=-1, keepdims=True)
    normed = (widened * lax.rsqrt(meansq + 1e-05) * norm_gain[0].astype(jnp.float32)).astype(
        jnp.bfloat16
    )
    cosine, sine = rotary_tables(positions[0])
    query = rotate(
        jnp.dot(normed, query_weight[0], preferred_element_type=jnp.float32), cosine, sine
    ).astype(jnp.bfloat16)
    keyval = jnp.dot(normed, key_value_weight[0], preferred_element_type=jnp.float32).astype(
        jnp.bfloat16
    )
    width = keyval.shape[1]
    shares = HEAD_WIDTH // width
    lane_share = jnp.arange(HEAD_WIDTH, dtype=jnp.int32) // width
    keyval = jnp.where(
        lane_share[None, :] == me % shares, jnp.tile(keyval, (1, shares)), jnp.bfloat16(0)
    )
    own = jnp.stack(
        [
            query.reshape(members, own_rows, HEAD_WIDTH),
            keyval.reshape(members, own_rows, HEAD_WIDTH),
        ],
        axis=1,
    )
    sent = jnp.broadcast_to(own[None], (groups,) + own.shape).reshape(
        (devices,) + own.shape[1:]
    )
    fresh = lax.all_to_all(sent, MINOR, 0, 0)
    queries = lax.dynamic_slice_in_dim(fresh[:, 0], group * members, members)
    fresh_key = lax.dynamic_slice_in_dim(fresh[:, 1], group * shares, shares)
    fresh_value = lax.dynamic_slice_in_dim(
        fresh[:, 1], devices // 2 + group * shares, shares
    )
    fresh_key = fresh_key.astype(jnp.float32).sum(0)
    fresh_value = fresh_value.astype(jnp.float32).sum(0)
    own_cosine = lax.dynamic_slice_in_dim(cosine, member * own_rows, own_rows)
    own_sine = lax.dynamic_slice_in_dim(sine, member * own_rows, own_rows)
    fresh_key = rotate(fresh_key, own_cosine, own_sine).astype(jnp.bfloat16)

    own_lengths = lax.dynamic_slice_in_dim(lengths[0], member * own_rows, own_rows)
    entries = devices * 2 * span * own_rows
    entry = jnp.arange(entries, dtype=jnp.int32)
    entry_row = entry % own_rows
    entry_slot = entry // (2 * span * own_rows) * span + entry // own_rows % span
    is_key = entry // (span * own_rows) % 2 == 0
    row_index = jnp.arange(own_rows, dtype=jnp.int32)[:, None]
    live = (is_key & (entry_row == row_index)) & (entry_slot < own_lengths[:, None])
    flat = stored.reshape(entries, HEAD_WIDTH)
    factor = 1.0 / math.sqrt(HEAD_WIDTH)
    scores = (
        lax.dot_general(
            queries, flat, (((2,), (1,)), ((), ())), preferred_element_type=jnp.float32
        )
        * factor
    )
    new_score = (queries.astype(jnp.float32) * fresh_key.astype(jnp.float32)).sum(-1) * factor
    scores = jnp.where(live, scores, -1e30)
    peak = jnp.maximum(scores.max(-1), new_score)
    weights = jnp.exp(scores - peak[..., None])
    new_weight = jnp.exp(new_score - peak)
    totals = weights.sum(-1) + new_weight
    mixture = lax.dot_general(
        jnp.roll(weights.astype(jnp.bfloat16), span * own_rows, axis=-1),
        flat,
        (((2,), (0,)), ((), ())),
        preferred_element_type=jnp.float32,
    )
    mixture = mixture + new_weight[..., None] * fresh_value
    attn = (mixture / totals[..., None]).astype(jnp.bfloat16)

    full = spread(attn.reshape(members * own_rows, HEAD_WIDTH))
    x, c, line = full.shape[:3]
    inner = members // c
    full = full.reshape(x, c, line // inner, inner, members, own_rows, HEAD_WIDTH)
    full = full.transpose(3, 1, 5, 0, 2, 4, 6).reshape(rows, -1)
    projected = jnp.dot(full, out_weight[0], preferred_element_type=jnp.float32)
    updated = (resid[0].astype(jnp.float32) + projected).astype(jnp.bfloat16)
    sections = lax.axis_size("section")
    following = [(i, (i + 1) % sections) for i in range(sections)]
    return lax.ppermute(updated, "section", following)[None]


def solution(mesh):
    sections, devices = mesh.devices.shape
    chips = devices // 4
    split = Mesh(
        mesh.devices.reshape(sections, 2, chips, 2), ("section",) + MINOR
    )
    return jax.shard_map(
        body,
        mesh=split,
        in_specs=(
            P("section", None, MINOR),
            P("section", None),
            P("section", None, MINOR),
            P("section", None, MINOR),
            P("section", None, MINOR),
            P("section", None, MINOR, None),
            P("section", None),
            P("section", None),
        ),
        out_specs=P("section", None, MINOR),
        check_vma=False,
    )
```

```python
import math

import jax
import jax.numpy as jnp
from jax import lax
from jax.sharding import Mesh
from jax.sharding import PartitionSpec as P

HEAD_WIDTH = 128
KEY_VALUE_HEADS = 8
MINOR = ("x", "z", "c")


def rotary_tables(token_positions):
    half_size = HEAD_WIDTH // 2
    freqs = jnp.exp(
        -math.log(500000.0) * 2.0 * jnp.arange(half_size, dtype=jnp.float32) / HEAD_WIDTH
    )
    angles = token_positions.astype(jnp.float32)[:, None] * freqs
    return jnp.cos(angles), jnp.sin(angles)


def rotate(vectors, cosine, sine):
    half_size = vectors.shape[-1] // 2
    first = vectors[..., :half_size]
    second = vectors[..., half_size:]
    return jnp.concatenate(
        [first * cosine - second * sine, second * cosine + first * sine], axis=-1
    )


def spread(part):
    line = lax.axis_size("z")
    copies = jnp.broadcast_to(part[None], (line,) + part.shape)
    along = lax.all_to_all(copies, "z", 0, 0)
    full = lax.all_gather(along, ("x", "c"))
    return full.reshape((lax.axis_size("x"), lax.axis_size("c"), line) + part.shape)


def body(
    resid,
    norm_gain,
    query_weight,
    key_value_weight,
    out_weight,
    key_value_cache,
    lengths,
    positions,
):
    rows = resid.shape[1]
    devices = lax.axis_size("x") * lax.axis_size("z") * lax.axis_size("c")
    groups = KEY_VALUE_HEADS
    members = devices // groups
    own_rows = rows // members
    me = lax.axis_index(MINOR)
    group, member = me // members, me % members
    span = key_value_cache.shape[2]

    pieces = key_value_cache[0].reshape(members, own_rows, span, 2, groups, HEAD_WIDTH)
    pieces = pieces.transpose(4, 0, 3, 2, 1, 5).reshape(
        groups, members, 2 * span * own_rows, HEAD_WIDTH
    )

    gathered = spread(resid[0])
    widened = gathered.transpose(3, 0, 2, 1, 4).reshape(rows, -1).astype(jnp.float32)
    meansq = jnp.mean(widened * widened, axis=-1, keepdims=True)
    normed = (widened * lax.rsqrt(meansq + 1e-05) * norm_gain[0].astype(jnp.float32)).astype(
        jnp.bfloat16
    )
    cosine, sine = rotary_tables(positions[0])
    query = rotate(
        jnp.dot(normed, query_weight[0], preferred_element_type=jnp.float32), cosine, sine
    ).astype(jnp.bfloat16)
    keyval = jnp.dot(normed, key_value_weight[0], preferred_element_type=jnp.float32).astype(
        jnp.bfloat16
    )
    width = keyval.shape[1]
    shares = HEAD_WIDTH // width
    lane_share = jnp.arange(HEAD_WIDTH, dtype=jnp.int32) // width
    keyval = jnp.where(
        lane_share[None, :] == me % shares, jnp.tile(keyval, (1, shares)), jnp.bfloat16(0)
    )
    own = jnp.concatenate(
        [
            query.reshape(members, own_rows, HEAD_WIDTH),
            keyval.reshape(members, own_rows, HEAD_WIDTH),
        ],
        axis=1,
    )
    sent = jnp.concatenate(
        [pieces, jnp.broadcast_to(own[None], (groups,) + own.shape)], axis=2
    ).reshape(devices, -1, 4, HEAD_WIDTH)
    arrived = lax.all_to_all(sent, MINOR, 0, 0).reshape(devices, -1, HEAD_WIDTH)
    per_device = arrived.shape[1]
    cached = 2 * span * own_rows
    fresh = arrived[:, cached:].reshape(devices, 2, own_rows, HEAD_WIDTH)
    queries = lax.dynamic_slice_in_dim(fresh[:, 0], group * members, members)
    fresh_key = lax.dynamic_slice_in_dim(fresh[:, 1], group * shares, shares)
    fresh_value = lax.dynamic_slice_in_dim(
        fresh[:, 1], devices // 2 + group * shares, shares
    )
    fresh_key = fresh_key.astype(jnp.float32).sum(0)
    fresh_value = fresh_value.astype(jnp.float32).sum(0)
    own_cosine = lax.dynamic_slice_in_dim(cosine, member * own_rows, own_rows)
    own_sine = lax.dynamic_slice_in_dim(sine, member * own_rows, own_rows)
    fresh_key = rotate(fresh_key, own_cosine, own_sine).astype(jnp.bfloat16)

    own_lengths = lax.dynamic_slice_in_dim(lengths[0], member * own_rows, own_rows)
    entries = devices * per_device
    entry = jnp.arange(entries, dtype=jnp.int32)
    entry_row = entry % own_rows
    entry_slot = entry // per_device * span + entry % per_device // own_rows
    is_key = entry % per_device < span * own_rows
    row_index = jnp.arange(own_rows, dtype=jnp.int32)[:, None]
    live = (is_key & (entry_row == row_index)) & (entry_slot < own_lengths[:, None])
    flat = arrived.reshape(entries, HEAD_WIDTH)
    factor = 1.0 / math.sqrt(HEAD_WIDTH)
    scores = (
        lax.dot_general(
            queries, flat, (((2,), (1,)), ((), ())), preferred_element_type=jnp.float32
        )
        * factor
    )
    new_score = (queries.astype(jnp.float32) * fresh_key.astype(jnp.float32)).sum(-1) * factor
    scores = jnp.where(live, scores, -1e30)
    peak = jnp.maximum(scores.max(-1), new_score)
    weights = jnp.exp(scores - peak[..., None])
    new_weight = jnp.exp(new_score - peak)
    totals = weights.sum(-1) + new_weight
    mixture = lax.dot_general(
        jnp.roll(weights.astype(jnp.bfloat16), span * own_rows, axis=-1),
        flat,
        (((2,), (0,)), ((), ())),
        preferred_element_type=jnp.float32,
    )
    mixture = mixture + new_weight[..., None] * fresh_value
    attn = (mixture / totals[..., None]).astype(jnp.bfloat16)

    full = spread(attn.reshape(members * own_rows, HEAD_WIDTH))
    x, c, line = full.shape[:3]
    inner = members // c
    full = full.reshape(x, c, line // inner, inner, members, own_rows, HEAD_WIDTH)
    full = full.transpose(3, 1, 5, 0, 2, 4, 6).reshape(rows, -1)
    projected = jnp.dot(full, out_weight[0], preferred_element_type=jnp.float32)
    updated = (resid[0].astype(jnp.float32) + projected).astype(jnp.bfloat16)
    sections = lax.axis_size("section")
    following = [(i, (i + 1) % sections) for i in range(sections)]
    return lax.ppermute(updated, "section", following)[None]


def solution(mesh):
    sections, devices = mesh.devices.shape
    chips = devices // 4
    split = Mesh(
        mesh.devices.reshape(sections, 2, chips, 2), ("section",) + MINOR
    )
    return jax.shard_map(
        body,
        mesh=split,
        in_specs=(
            P("section", None, MINOR),
            P("section", None),
            P("section", None, MINOR),
            P("section", None, MINOR),
            P("section", None, MINOR),
            P("section", None, MINOR, None),
            P("section", None),
            P("section", None),
        ),
        out_specs=P("section", None, MINOR),
        check_vma=False,
    )
```

```python
import functools
import math

import jax
import jax.numpy as jnp
from jax import lax
from jax.experimental import pallas as pl
from jax.experimental.pallas import tpu as pltpu
from jax.sharding import Mesh
from jax.sharding import PartitionSpec as P

HEAD_WIDTH = 128
KEY_VALUE_HEADS = 8
MINOR = ("x", "z", "c")


def rotary_tables(token_positions):
    half_size = HEAD_WIDTH // 2
    freqs = jnp.exp(
        -math.log(500000.0) * 2.0 * jnp.arange(half_size, dtype=jnp.float32) / HEAD_WIDTH
    )
    angles = token_positions.astype(jnp.float32)[:, None] * freqs
    return jnp.cos(angles), jnp.sin(angles)


def rotate(vectors, cosine, sine):
    half_size = vectors.shape[-1] // 2
    first = vectors[..., :half_size]
    second = vectors[..., half_size:]
    return jnp.concatenate(
        [first * cosine - second * sine, second * cosine + first * sine], axis=-1
    )


def spread(part):
    line = lax.axis_size("z")
    copies = jnp.broadcast_to(part[None], (line,) + part.shape)
    along = lax.all_to_all(copies, "z", 0, 0)
    full = lax.all_gather(along, ("x", "c"))
    return full.reshape((lax.axis_size("x"), lax.axis_size("c"), line) + part.shape)


def place_rows(cores, line, gathered_ref, gain_ref, query_ref, keyval_ref, cosine_ref, sine_ref,
               share_ref, out_ref, normed_ref):
    rows, width = gathered_ref.shape[1:]
    squares = jnp.zeros((rows, width), jnp.float32)
    for at in range(gathered_ref.shape[0]):
        wide = gathered_ref[at].astype(jnp.float32)
        squares = squares + wide * wide
    meansq = jnp.sum(squares, axis=-1, keepdims=True) / (gathered_ref.shape[0] * width)
    scale = lax.rsqrt(meansq + 1e-05)
    for at in range(gathered_ref.shape[0]):
        side, core, chip = at // (cores * line), at // line % cores, at % line
        first = ((side * line + chip) * cores + core) * width
        gain = gain_ref[:, first : first + width].astype(jnp.float32)
        wide = gathered_ref[at].astype(jnp.float32)
        normed_ref[:, first : first + width] = (wide * scale * gain).astype(jnp.bfloat16)
    normed = normed_ref[...]
    query = jnp.dot(normed, query_ref[...], preferred_element_type=jnp.float32)
    keyval = lax.dot_general(
        normed, keyval_ref[...], (((1,), (1,)), ((), ())), preferred_element_type=jnp.float32
    ).astype(jnp.bfloat16)
    query = query * cosine_ref[...] + pltpu.roll(query, width // 2, 1) * sine_ref[...]
    part = keyval.shape[1]
    lane = lax.broadcasted_iota(jnp.int32, (part, width), 1)
    column = lax.broadcasted_iota(jnp.int32, (part, width), 0)
    place = jnp.where(lane == column + share_ref[0] * part, 1.0, 0.0).astype(jnp.bfloat16)
    placed = jnp.dot(keyval, place, preferred_element_type=jnp.float32).astype(jnp.bfloat16)
    both = jnp.concatenate([query.astype(jnp.bfloat16), placed], axis=0)
    to = lax.broadcasted_iota(jnp.int32, (2 * rows, 2 * rows), 0)
    source = lax.broadcasted_iota(jnp.int32, (2 * rows, 2 * rows), 1)
    wanted = (to // 4) * 2 + to % 2 + jnp.where(to % 4 >= 2, rows, 0)
    order = jnp.where(source == wanted, 1.0, 0.0).astype(jnp.bfloat16)
    out_ref[...] = jnp.dot(order, both, preferred_element_type=jnp.float32).astype(jnp.bfloat16)


def add_product(attn_ref, weight_ref, resid_ref, out_ref):
    product = jnp.dot(attn_ref[...], weight_ref[...], preferred_element_type=jnp.float32)
    out_ref[...] = (resid_ref[...].astype(jnp.float32) + product).astype(out_ref.dtype)


def body(
    resid,
    norm_gain,
    query_weight,
    key_value_weight,
    out_weight,
    key_value_cache,
    lengths,
    positions,
):
    rows = resid.shape[1]
    devices = lax.axis_size("x") * lax.axis_size("z") * lax.axis_size("c")
    groups = KEY_VALUE_HEADS
    members = devices // groups
    own_rows = rows // members
    me = lax.axis_index(MINOR)
    group, member = me // members, me % members
    span = key_value_cache.shape[2]

    pieces = key_value_cache[0].reshape(members, own_rows, span, 2, groups, HEAD_WIDTH)
    pieces = pieces.transpose(4, 0, 3, 2, 1, 5).reshape(
        devices, span, 2 * own_rows, HEAD_WIDTH
    )
    pieces = lax.optimization_barrier(jnp.pad(pieces, ((0, 0), (0, 1), (0, 0), (0, 0))))

    gathered = spread(resid[0])
    side, cores, line = gathered.shape[:3]
    cosine, sine = rotary_tables(positions[0])
    width = key_value_weight.shape[2]
    shares = HEAD_WIDTH // width
    whole, small = pl.BlockSpec(memory_space=pltpu.VMEM), pl.BlockSpec(memory_space=pltpu.SMEM)
    own = pl.pallas_call(
        functools.partial(place_rows, cores, line),
        out_shape=jax.ShapeDtypeStruct((2 * rows, HEAD_WIDTH), jnp.bfloat16),
        in_specs=[whole] * 6 + [small],
        out_specs=whole,
        scratch_shapes=[pltpu.VMEM((rows, query_weight.shape[1]), jnp.bfloat16)],
        compiler_params=pltpu.CompilerParams(vmem_limit_bytes=24 * 2**20),
    )(
        gathered.reshape((devices,) + resid.shape[1:]),
        norm_gain,
        query_weight[0],
        key_value_weight[0].T,
        jnp.concatenate([cosine, cosine], axis=1),
        jnp.concatenate([-sine, sine], axis=1),
        (me % shares).reshape(1),
    )
    own = own.reshape(members, 2 * own_rows, HEAD_WIDTH)
    own = jnp.broadcast_to(own[None], (groups,) + own.shape).reshape(
        devices, 1, 2 * own_rows, HEAD_WIDTH
    )
    sent = lax.dynamic_update_slice_in_dim(pieces, own, pieces.shape[1] - 1, axis=1)
    arrived = lax.all_to_all(sent, MINOR, 0, 0).reshape(devices, -1, HEAD_WIDTH)
    per_device = arrived.shape[1]
    cached = 2 * span * own_rows
    fresh = arrived[:, cached:].reshape(devices, 2, own_rows, HEAD_WIDTH)
    queries = lax.dynamic_slice_in_dim(fresh[:, 0], group * members, members)
    fresh_key = lax.dynamic_slice_in_dim(fresh[:, 1], group * shares, shares)
    fresh_value = lax.dynamic_slice_in_dim(
        fresh[:, 1], devices // 2 + group * shares, shares
    )
    fresh_key = fresh_key.astype(jnp.float32).sum(0)
    fresh_value = fresh_value.astype(jnp.float32).sum(0)
    own_cosine = lax.dynamic_slice_in_dim(cosine, member * own_rows, own_rows)
    own_sine = lax.dynamic_slice_in_dim(sine, member * own_rows, own_rows)
    fresh_key = rotate(fresh_key, own_cosine, own_sine).astype(jnp.bfloat16)

    own_lengths = lax.dynamic_slice_in_dim(lengths[0], member * own_rows, own_rows)
    entries = devices * per_device
    entry = jnp.arange(entries, dtype=jnp.int32)
    entry_row = entry % own_rows
    entry_slot = entry // per_device * span + entry % per_device // own_rows
    is_key = entry % per_device < span * own_rows
    row_index = jnp.arange(own_rows, dtype=jnp.int32)[:, None]
    live = (is_key & (entry_row == row_index)) & (entry_slot < own_lengths[:, None])
    flat = arrived.reshape(entries, HEAD_WIDTH)
    factor = 1.0 / math.sqrt(HEAD_WIDTH)
    scores = (
        lax.dot_general(
            queries, flat, (((2,), (1,)), ((), ())), preferred_element_type=jnp.float32
        )
        * factor
    )
    new_score = (queries.astype(jnp.float32) * fresh_key.astype(jnp.float32)).sum(-1) * factor
    scores = jnp.where(live, scores, -1e30)
    peak = jnp.maximum(scores.max(-1), new_score)
    weights = jnp.exp(scores - peak[..., None])
    new_weight = jnp.exp(new_score - peak)
    totals = weights.sum(-1) + new_weight
    mixture = lax.dot_general(
        jnp.roll(weights.astype(jnp.bfloat16), span * own_rows, axis=-1),
        flat,
        (((2,), (0,)), ((), ())),
        preferred_element_type=jnp.float32,
    )
    mixture = mixture + new_weight[..., None] * fresh_value
    attn = (mixture / totals[..., None]).astype(jnp.bfloat16)

    full = spread(attn.reshape(members * own_rows, HEAD_WIDTH))
    x, c, line = full.shape[:3]
    inner = members // c
    full = full.reshape(x, c, line // inner, inner, members, own_rows, HEAD_WIDTH)
    full = full.transpose(3, 1, 5, 0, 2, 4, 6).reshape(rows, -1)
    updated = pl.pallas_call(
        add_product,
        out_shape=jax.ShapeDtypeStruct(resid.shape[1:], resid.dtype),
        in_specs=[whole] * 3,
        out_specs=whole,
        compiler_params=pltpu.CompilerParams(vmem_limit_bytes=24 * 2**20),
    )(full, out_weight[0], resid[0])
    sections = lax.axis_size("section")
    following = [(i, (i + 1) % sections) for i in range(sections)]
    return lax.ppermute(updated, "section", following)[None]


def solution(mesh):
    sections, devices = mesh.devices.shape
    chips = devices // 4
    split = Mesh(
        mesh.devices.reshape(sections, 2, chips, 2), ("section",) + MINOR
    )
    return jax.shard_map(
        body,
        mesh=split,
        in_specs=(
            P("section", None, MINOR),
            P("section", None),
            P("section", None, MINOR),
            P("section", None, MINOR),
            P("section", None, MINOR),
            P("section", None, MINOR, None),
            P("section", None),
            P("section", None),
        ),
        out_specs=P("section", None, MINOR),
        check_vma=False,
    )
```

```python
import functools
import math

import jax
import jax.numpy as jnp
from jax import lax
from jax.experimental import pallas as pl
from jax.experimental.pallas import tpu as pltpu
from jax.sharding import Mesh
from jax.sharding import PartitionSpec as P

HEAD_WIDTH = 128
KEY_VALUE_HEADS = 8
MINOR = ("x", "z", "c")


def rotary_tables(token_positions):
    half_size = HEAD_WIDTH // 2
    freqs = jnp.exp(
        -math.log(500000.0) * 2.0 * jnp.arange(half_size, dtype=jnp.float32) / HEAD_WIDTH
    )
    angles = token_positions.astype(jnp.float32)[:, None] * freqs
    return jnp.cos(angles), jnp.sin(angles)


def spread(part):
    line = lax.axis_size("z")
    copies = jnp.broadcast_to(part[None], (line,) + part.shape)
    along = lax.all_to_all(copies, "z", 0, 0)
    full = lax.all_gather(along, ("x", "c"))
    return full.reshape((lax.axis_size("x"), lax.axis_size("c"), line) + part.shape)


def place_rows(cores, line, gathered_ref, gain_ref, query_ref, keyval_ref, cosine_ref, sine_ref,
               share_ref, out_ref, normed_ref):
    rows, width = gathered_ref.shape[1:]
    squares = jnp.zeros((rows, width), jnp.float32)
    for at in range(gathered_ref.shape[0]):
        wide = gathered_ref[at].astype(jnp.float32)
        squares = squares + wide * wide
    meansq = jnp.sum(squares, axis=-1, keepdims=True) / (gathered_ref.shape[0] * width)
    scale = lax.rsqrt(meansq + 1e-05)
    for at in range(gathered_ref.shape[0]):
        side, core, chip = at // (cores * line), at // line % cores, at % line
        first = ((side * line + chip) * cores + core) * width
        gain = gain_ref[:, first : first + width].astype(jnp.float32)
        wide = gathered_ref[at].astype(jnp.float32)
        normed_ref[:, first : first + width] = (wide * scale * gain).astype(jnp.bfloat16)
    normed = normed_ref[...]
    query = jnp.dot(normed, query_ref[...], preferred_element_type=jnp.float32)
    keyval = lax.dot_general(
        normed, keyval_ref[...], (((1,), (1,)), ((), ())), preferred_element_type=jnp.float32
    ).astype(jnp.bfloat16)
    query = query * cosine_ref[...] + pltpu.roll(query, width // 2, 1) * sine_ref[...]
    part = keyval.shape[1]
    lane = lax.broadcasted_iota(jnp.int32, (part, width), 1)
    column = lax.broadcasted_iota(jnp.int32, (part, width), 0)
    place = jnp.where(lane == column + share_ref[0] * part, 1.0, 0.0).astype(jnp.bfloat16)
    placed = jnp.dot(keyval, place, preferred_element_type=jnp.float32).astype(jnp.bfloat16)
    both = jnp.concatenate([query.astype(jnp.bfloat16), placed], axis=0)
    to = lax.broadcasted_iota(jnp.int32, (2 * rows, 2 * rows), 0)
    source = lax.broadcasted_iota(jnp.int32, (2 * rows, 2 * rows), 1)
    wanted = (to // 4) * 2 + to % 2 + jnp.where(to % 4 >= 2, rows, 0)
    order = jnp.where(source == wanted, 1.0, 0.0).astype(jnp.bfloat16)
    out_ref[...] = jnp.dot(order, both, preferred_element_type=jnp.float32).astype(jnp.bfloat16)


def attend(span, factor, entries_ref, select_ref, bias_ref, cosine_ref, sine_ref, out_ref):
    entries = entries_ref[...]
    rows, width = out_ref.shape
    picked = jnp.dot(select_ref[...], entries, preferred_element_type=jnp.float32)
    query, fresh_key, fresh_value = picked[:rows], picked[rows : 2 * rows], picked[2 * rows :]
    scores = lax.dot_general(
        query.astype(jnp.bfloat16),
        entries,
        (((1,), (1,)), ((), ())),
        preferred_element_type=jnp.float32,
    )
    scores = scores * factor + bias_ref[...]
    fresh_key = fresh_key * cosine_ref[...] + pltpu.roll(fresh_key, width // 2, 1) * sine_ref[...]
    fresh_key = fresh_key.astype(jnp.bfloat16).astype(jnp.float32)
    new_score = jnp.sum(query * fresh_key, axis=-1, keepdims=True) * factor
    peak = jnp.maximum(jnp.max(scores, axis=-1, keepdims=True), new_score)
    weights = jnp.exp(scores - peak)
    new_weight = jnp.exp(new_score - peak)
    totals = jnp.sum(weights, axis=-1, keepdims=True) + new_weight
    weights = pltpu.roll(weights, span, 1).astype(jnp.bfloat16)
    mixture = jnp.dot(weights, entries, preferred_element_type=jnp.float32)
    mixture = mixture + new_weight * fresh_value
    out_ref[...] = (mixture / totals).astype(jnp.bfloat16)


def add_product(attn_ref, weight_ref, resid_ref, out_ref):
    product = jnp.dot(attn_ref[...], weight_ref[...], preferred_element_type=jnp.float32)
    out_ref[...] = (resid_ref[...].astype(jnp.float32) + product).astype(out_ref.dtype)


def body(
    resid,
    norm_gain,
    query_weight,
    key_value_weight,
    out_weight,
    key_value_cache,
    lengths,
    positions,
):
    rows = resid.shape[1]
    devices = lax.axis_size("x") * lax.axis_size("z") * lax.axis_size("c")
    groups = KEY_VALUE_HEADS
    members = devices // groups
    own_rows = rows // members
    me = lax.axis_index(MINOR)
    group, member = me // members, me % members
    span = key_value_cache.shape[2]

    pieces = key_value_cache[0].reshape(members, own_rows, span, 2, groups, HEAD_WIDTH)
    pieces = pieces.transpose(4, 0, 3, 2, 1, 5).reshape(
        devices, span, 2 * own_rows, HEAD_WIDTH
    )
    pieces = lax.optimization_barrier(jnp.pad(pieces, ((0, 0), (0, 1), (0, 0), (0, 0))))

    gathered = spread(resid[0])
    side, cores, line = gathered.shape[:3]
    cosine, sine = rotary_tables(positions[0])
    width = key_value_weight.shape[2]
    shares = HEAD_WIDTH // width
    whole, small = pl.BlockSpec(memory_space=pltpu.VMEM), pl.BlockSpec(memory_space=pltpu.SMEM)
    own = pl.pallas_call(
        functools.partial(place_rows, cores, line),
        out_shape=jax.ShapeDtypeStruct((2 * rows, HEAD_WIDTH), jnp.bfloat16),
        in_specs=[whole] * 6 + [small],
        out_specs=whole,
        scratch_shapes=[pltpu.VMEM((rows, query_weight.shape[1]), jnp.bfloat16)],
        compiler_params=pltpu.CompilerParams(vmem_limit_bytes=24 * 2**20),
    )(
        gathered.reshape((devices,) + resid.shape[1:]),
        norm_gain,
        query_weight[0],
        key_value_weight[0].T,
        jnp.concatenate([cosine, cosine], axis=1),
        jnp.concatenate([-sine, sine], axis=1),
        (me % shares).reshape(1),
    )
    own = own.reshape(members, 2 * own_rows, HEAD_WIDTH)
    own = jnp.broadcast_to(own[None], (groups,) + own.shape).reshape(
        devices, 1, 2 * own_rows, HEAD_WIDTH
    )
    sent = lax.dynamic_update_slice_in_dim(pieces, own, pieces.shape[1] - 1, axis=1)
    arrived = lax.all_to_all(sent, MINOR, 0, 0).reshape(devices, -1, HEAD_WIDTH)
    per_device = arrived.shape[1]
    cached = 2 * span * own_rows
    entries = devices * per_device

    own_lengths = lax.dynamic_slice_in_dim(lengths[0], member * own_rows, own_rows)
    own_cosine = lax.dynamic_slice_in_dim(cosine, member * own_rows, own_rows)
    own_sine = lax.dynamic_slice_in_dim(sine, member * own_rows, own_rows)
    entry = jnp.arange(entries, dtype=jnp.int32)
    entry_from, entry_at = entry // per_device, entry % per_device
    entry_row = entry_at % own_rows
    entry_slot = entry_from * span + entry_at // own_rows
    rank = jnp.arange(members * own_rows, dtype=jnp.int32)[:, None]
    rank_row = rank % own_rows
    is_query = (entry_at >= cached) & (entry_at < cached + own_rows)
    is_fresh = entry_at >= cached + own_rows
    select = [
        is_query & (entry_from == group * members + rank // own_rows),
        is_fresh & (entry_from // shares == group),
        is_fresh & (entry_from // shares == groups + group),
    ]
    select = jnp.concatenate([part & (entry_row == rank_row) for part in select]).astype(
        jnp.bfloat16
    )
    live = (entry_at < span * own_rows) & (entry_row == rank_row)
    live = live & (entry_slot < jnp.tile(own_lengths, members)[:, None])
    bias = jnp.where(live, 0.0, -1e30)
    attn = pl.pallas_call(
        functools.partial(attend, span * own_rows, 1.0 / math.sqrt(HEAD_WIDTH)),
        out_shape=jax.ShapeDtypeStruct((members * own_rows, HEAD_WIDTH), jnp.bfloat16),
        in_specs=[whole] * 5,
        out_specs=whole,
        compiler_params=pltpu.CompilerParams(vmem_limit_bytes=24 * 2**20),
    )(
        arrived.reshape(entries, HEAD_WIDTH),
        select,
        bias,
        jnp.tile(jnp.concatenate([own_cosine, own_cosine], axis=1), (members, 1)),
        jnp.tile(jnp.concatenate([-own_sine, own_sine], axis=1), (members, 1)),
    )

    full = spread(attn)
    x, c, line = full.shape[:3]
    inner = members // c
    full = full.reshape(x, c, line // inner, inner, members, own_rows, HEAD_WIDTH)
    full = full.transpose(3, 1, 5, 0, 2, 4, 6).reshape(rows, -1)
    updated = pl.pallas_call(
        add_product,
        out_shape=jax.ShapeDtypeStruct(resid.shape[1:], resid.dtype),
        in_specs=[whole] * 3,
        out_specs=whole,
        compiler_params=pltpu.CompilerParams(vmem_limit_bytes=24 * 2**20),
    )(full, out_weight[0], resid[0])
    sections = lax.axis_size("section")
    following = [(i, (i + 1) % sections) for i in range(sections)]
    return lax.ppermute(updated, "section", following)[None]


def solution(mesh):
    sections, devices = mesh.devices.shape
    chips = devices // 4
    split = Mesh(
        mesh.devices.reshape(sections, 2, chips, 2), ("section",) + MINOR
    )
    return jax.shard_map(
        body,
        mesh=split,
        in_specs=(
            P("section", None, MINOR),
            P("section", None),
            P("section", None, MINOR),
            P("section", None, MINOR),
            P("section", None, MINOR),
            P("section", None, MINOR, None),
            P("section", None),
            P("section", None),
        ),
        out_specs=P("section", None, MINOR),
        check_vma=False,
    )
```

```python
import functools
import math

import jax
import jax.numpy as jnp
from jax import lax
from jax.experimental import pallas as pl
from jax.experimental.pallas import tpu as pltpu
from jax.sharding import Mesh
from jax.sharding import PartitionSpec as P

HEAD_WIDTH = 128
KEY_VALUE_HEADS = 8
LINE = ("za", "zb")
MINOR = ("x",) + LINE + ("c",)


def rotary_tables(token_positions):
    half_size = HEAD_WIDTH // 2
    freqs = jnp.exp(
        -math.log(500000.0) * 2.0 * jnp.arange(half_size, dtype=jnp.float32) / HEAD_WIDTH
    )
    angles = token_positions.astype(jnp.float32)[:, None] * freqs
    return jnp.cos(angles), jnp.sin(angles)


def spread(part):
    line = lax.axis_size(LINE)
    copies = jnp.broadcast_to(part[None], (line,) + part.shape)
    along = lax.all_to_all(copies, LINE, 0, 0)
    full = lax.all_gather(along, ("x", "c"))
    return full.reshape((lax.axis_size("x"), lax.axis_size("c"), line) + part.shape)


def place_rows(cores, line, gathered_ref, gain_ref, query_ref, keyval_ref, cosine_ref, sine_ref,
               share_ref, out_ref, near_ref, normed_ref):
    rows, width = gathered_ref.shape[1:]
    squares = jnp.zeros((rows, width), jnp.float32)
    for at in range(gathered_ref.shape[0]):
        wide = gathered_ref[at].astype(jnp.float32)
        squares = squares + wide * wide
    meansq = jnp.sum(squares, axis=-1, keepdims=True) / (gathered_ref.shape[0] * width)
    scale = lax.rsqrt(meansq + 1e-05)
    for at in range(gathered_ref.shape[0]):
        side, core, chip = at // (cores * line), at // line % cores, at % line
        first = ((side * line + chip) * cores + core) * width
        gain = gain_ref[:, first : first + width].astype(jnp.float32)
        wide = gathered_ref[at].astype(jnp.float32)
        normed_ref[:, first : first + width] = (wide * scale * gain).astype(jnp.bfloat16)
    normed = normed_ref[...]
    query = jnp.dot(normed, query_ref[...], preferred_element_type=jnp.float32)
    keyval = lax.dot_general(
        normed, keyval_ref[...], (((1,), (1,)), ((), ())), preferred_element_type=jnp.float32
    ).astype(jnp.bfloat16)
    query = query * cosine_ref[...] + pltpu.roll(query, width // 2, 1) * sine_ref[...]
    part = keyval.shape[1]
    lane = lax.broadcasted_iota(jnp.int32, (part, width), 1)
    column = lax.broadcasted_iota(jnp.int32, (part, width), 0)
    place = jnp.where(lane == column + share_ref[0] * part, 1.0, 0.0).astype(jnp.bfloat16)
    placed = jnp.dot(keyval, place, preferred_element_type=jnp.float32)
    near_ref[...] = placed.astype(jnp.bfloat16)
    out_ref[...] = query.astype(jnp.bfloat16)


def attend(span, factor, entries_ref, near_ref, select_ref, near_select_ref, bias_ref, cosine_ref,
           sine_ref, out_ref):
    entries = entries_ref[...]
    rows, width = out_ref.shape
    picked = jnp.dot(select_ref[...], entries, preferred_element_type=jnp.float32)
    query = jnp.dot(near_select_ref[...], near_ref[...], preferred_element_type=jnp.float32)
    fresh_key, fresh_value = picked[:rows], picked[rows:]
    scores = lax.dot_general(
        query.astype(jnp.bfloat16),
        entries,
        (((1,), (1,)), ((), ())),
        preferred_element_type=jnp.float32,
    )
    scores = scores * factor + bias_ref[...]
    fresh_key = fresh_key * cosine_ref[...] + pltpu.roll(fresh_key, width // 2, 1) * sine_ref[...]
    fresh_key = fresh_key.astype(jnp.bfloat16).astype(jnp.float32)
    new_score = jnp.sum(query * fresh_key, axis=-1, keepdims=True) * factor
    peak = jnp.maximum(jnp.max(scores, axis=-1, keepdims=True), new_score)
    weights = jnp.exp(scores - peak)
    new_weight = jnp.exp(new_score - peak)
    totals = jnp.sum(weights, axis=-1, keepdims=True) + new_weight
    weights = pltpu.roll(weights, span, 1).astype(jnp.bfloat16)
    mixture = jnp.dot(weights, entries, preferred_element_type=jnp.float32)
    mixture = mixture + new_weight * fresh_value
    out_ref[...] = (mixture / totals).astype(jnp.bfloat16)


def add_product(attn_ref, weight_ref, resid_ref, out_ref):
    product = jnp.dot(attn_ref[...], weight_ref[...], preferred_element_type=jnp.float32)
    out_ref[...] = (resid_ref[...].astype(jnp.float32) + product).astype(out_ref.dtype)


def body(
    resid,
    norm_gain,
    query_weight,
    key_value_weight,
    out_weight,
    key_value_cache,
    lengths,
    positions,
):
    rows = resid.shape[1]
    devices = lax.axis_size(MINOR)
    groups = KEY_VALUE_HEADS
    members = devices // groups
    own_rows = rows // members
    me = lax.axis_index(MINOR)
    group, member = me // members, me % members
    span = key_value_cache.shape[2]

    pieces = key_value_cache[0].reshape(members, own_rows, span, 2, groups, HEAD_WIDTH)
    pieces = pieces.transpose(4, 0, 3, 2, 1, 5).reshape(
        devices, 2 * span, own_rows, HEAD_WIDTH
    )
    pieces = lax.optimization_barrier(jnp.pad(pieces, ((0, 0), (0, 1), (0, 0), (0, 0))))

    gathered = spread(resid[0])
    side, cores, line = gathered.shape[:3]
    cosine, sine = rotary_tables(positions[0])
    width = key_value_weight.shape[2]
    shares = HEAD_WIDTH // width
    whole, small = pl.BlockSpec(memory_space=pltpu.VMEM), pl.BlockSpec(memory_space=pltpu.SMEM)
    query, fresh = pl.pallas_call(
        functools.partial(place_rows, cores, line),
        out_shape=(
            jax.ShapeDtypeStruct((rows, HEAD_WIDTH), jnp.bfloat16),
            jax.ShapeDtypeStruct((rows, HEAD_WIDTH), jnp.bfloat16),
        ),
        in_specs=[whole] * 6 + [small],
        out_specs=(whole, whole),
        scratch_shapes=[pltpu.VMEM((rows, query_weight.shape[1]), jnp.bfloat16)],
        compiler_params=pltpu.CompilerParams(vmem_limit_bytes=24 * 2**20),
    )(
        gathered.reshape((devices,) + resid.shape[1:]),
        norm_gain,
        query_weight[0],
        key_value_weight[0].T,
        jnp.concatenate([cosine, cosine], axis=1),
        jnp.concatenate([-sine, sine], axis=1),
        (me % shares).reshape(1),
    )
    fresh = jnp.broadcast_to(fresh[None], (groups,) + fresh.shape)
    fresh = fresh.reshape(devices, 1, own_rows, HEAD_WIDTH)
    sent = lax.dynamic_update_slice_in_dim(pieces, fresh, pieces.shape[1] - 1, axis=1)
    arrived = lax.all_to_all(sent, MINOR, 0, 0).reshape(devices, -1, HEAD_WIDTH)
    chip = lax.all_gather(query, "c")
    chips = lax.axis_size("zb")
    near = [chip] + [
        lax.ppermute(chip, "zb", [(i, (i + by) % chips) for i in range(chips)])
        for by in range(1, chips)
    ]
    near = jnp.stack(near).reshape(members * rows, HEAD_WIDTH)
    per_device = arrived.shape[1]
    cached = 2 * span * own_rows
    entries = devices * per_device

    own_lengths = lax.dynamic_slice_in_dim(lengths[0], member * own_rows, own_rows)
    own_cosine = lax.dynamic_slice_in_dim(cosine, member * own_rows, own_rows)
    own_sine = lax.dynamic_slice_in_dim(sine, member * own_rows, own_rows)
    entry = jnp.arange(entries, dtype=jnp.int32)
    entry_from, entry_at = entry // per_device, entry % per_device
    entry_row = entry_at % own_rows
    entry_slot = entry_from * span + entry_at // own_rows
    rank = jnp.arange(members * own_rows, dtype=jnp.int32)[:, None]
    rank_row = rank % own_rows
    holders = [group * shares, devices // 2 + group * shares]
    select = jnp.concatenate(
        [
            (entry_at >= cached) & (entry_from // shares == holder // shares)
            & (entry_row == rank_row)
            for holder in holders
        ]
    ).astype(jnp.bfloat16)
    near_at = jnp.arange(members * rows, dtype=jnp.int32)
    per_chip = rows * members // chips
    near_chip = (lax.axis_index("zb") - near_at // per_chip) % chips
    near_from = near_chip * (members // chips) + near_at % per_chip // rows
    near_select = (near_from == rank // own_rows) & (
        near_at % rows == member * own_rows + rank_row
    )
    near_select = near_select.astype(jnp.bfloat16)
    live = (entry_at < span * own_rows) & (entry_row == rank_row)
    live = live & (entry_slot < jnp.tile(own_lengths, members)[:, None])
    bias = jnp.where(live, 0.0, -1e30)
    attn = pl.pallas_call(
        functools.partial(attend, span * own_rows, 1.0 / math.sqrt(HEAD_WIDTH)),
        out_shape=jax.ShapeDtypeStruct((members * own_rows, HEAD_WIDTH), jnp.bfloat16),
        in_specs=[whole] * 7,
        out_specs=whole,
        compiler_params=pltpu.CompilerParams(vmem_limit_bytes=24 * 2**20),
    )(
        arrived.reshape(entries, HEAD_WIDTH),
        near,
        select,
        near_select,
        bias,
        jnp.tile(jnp.concatenate([own_cosine, own_cosine], axis=1), (members, 1)),
        jnp.tile(jnp.concatenate([-own_sine, own_sine], axis=1), (members, 1)),
    )

    full = spread(attn)
    x, c, line = full.shape[:3]
    inner = members // c
    full = full.reshape(x, c, line // inner, inner, members, own_rows, HEAD_WIDTH)
    full = full.transpose(3, 1, 5, 0, 2, 4, 6).reshape(rows, -1)
    updated = pl.pallas_call(
        add_product,
        out_shape=jax.ShapeDtypeStruct(resid.shape[1:], resid.dtype),
        in_specs=[whole] * 3,
        out_specs=whole,
        compiler_params=pltpu.CompilerParams(vmem_limit_bytes=24 * 2**20),
    )(full, out_weight[0], resid[0])
    sections = lax.axis_size("section")
    following = [(i, (i + 1) % sections) for i in range(sections)]
    return lax.ppermute(updated, "section", following)[None]


def solution(mesh):
    sections, devices = mesh.devices.shape
    near = devices // KEY_VALUE_HEADS // 2
    split = Mesh(
        mesh.devices.reshape(sections, 2, devices // (4 * near), near, 2), ("section",) + MINOR
    )
    return jax.shard_map(
        body,
        mesh=split,
        in_specs=(
            P("section", None, MINOR),
            P("section", None),
            P("section", None, MINOR),
            P("section", None, MINOR),
            P("section", None, MINOR),
            P("section", None, MINOR, None),
            P("section", None),
            P("section", None),
        ),
        out_specs=P("section", None, MINOR),
        check_vma=False,
    )
```

```python
import functools
import math

import jax
import jax.numpy as jnp
from jax import lax
from jax.experimental import pallas as pl
from jax.experimental.pallas import tpu as pltpu
from jax.sharding import Mesh
from jax.sharding import PartitionSpec as P

HEAD_WIDTH = 128
KEY_VALUE_HEADS = 8
LINE = ("za", "zb")
MINOR = ("x",) + LINE + ("c",)


def rotary_tables(token_positions):
    half_size = HEAD_WIDTH // 2
    freqs = jnp.exp(
        -math.log(500000.0) * 2.0 * jnp.arange(half_size, dtype=jnp.float32) / HEAD_WIDTH
    )
    angles = token_positions.astype(jnp.float32)[:, None] * freqs
    return jnp.cos(angles), jnp.sin(angles)


def spread(part):
    line = lax.axis_size(LINE)
    copies = jnp.broadcast_to(part[None], (line,) + part.shape)
    along = lax.all_to_all(copies, LINE, 0, 0)
    full = lax.all_gather(along, ("x", "c"))
    return full.reshape((lax.axis_size("x"), lax.axis_size("c"), line) + part.shape)


def place_rows(cores, line, gathered_ref, gain_ref, keyval_ref, share_ref, fresh_ref, normed_ref):
    rows, width = gathered_ref.shape[1:]
    squares = jnp.zeros((rows, width), jnp.float32)
    for at in range(gathered_ref.shape[0]):
        wide = gathered_ref[at].astype(jnp.float32)
        squares = squares + wide * wide
    meansq = jnp.sum(squares, axis=-1, keepdims=True) / (gathered_ref.shape[0] * width)
    scale = lax.rsqrt(meansq + 1e-05)
    for at in range(gathered_ref.shape[0]):
        side, core, chip = at // (cores * line), at // line % cores, at % line
        first = ((side * line + chip) * cores + core) * width
        gain = gain_ref[:, first : first + width].astype(jnp.float32)
        wide = gathered_ref[at].astype(jnp.float32)
        normed_ref[:, first : first + width] = (wide * scale * gain).astype(jnp.bfloat16)
    keyval = lax.dot_general(
        normed_ref[...],
        keyval_ref[...],
        (((1,), (1,)), ((), ())),
        preferred_element_type=jnp.float32,
    ).astype(jnp.bfloat16)
    part = keyval.shape[1]
    lane = lax.broadcasted_iota(jnp.int32, (part, width), 1)
    column = lax.broadcasted_iota(jnp.int32, (part, width), 0)
    place = jnp.where(lane == column + share_ref[0] * part, 1.0, 0.0).astype(jnp.bfloat16)
    placed = jnp.dot(keyval, place, preferred_element_type=jnp.float32)
    fresh_ref[...] = placed.astype(jnp.bfloat16)


def rotate_query(normed_ref, query_ref, cosine_ref, sine_ref, out_ref):
    query = jnp.dot(normed_ref[...], query_ref[...], preferred_element_type=jnp.float32)
    turned = pltpu.roll(query, query.shape[1] // 2, 1)
    query = query * cosine_ref[...] + turned * sine_ref[...]
    out_ref[...] = query.astype(jnp.bfloat16)


def attend(span, factor, entries_ref, near_ref, select_ref, near_select_ref, bias_ref, cosine_ref,
           sine_ref, out_ref):
    entries = entries_ref[...]
    rows, width = out_ref.shape
    picked = jnp.dot(select_ref[...], entries, preferred_element_type=jnp.float32)
    query = jnp.dot(near_select_ref[...], near_ref[...], preferred_element_type=jnp.float32)
    fresh_key, fresh_value = picked[:rows], picked[rows:]
    scores = lax.dot_general(
        query.astype(jnp.bfloat16),
        entries,
        (((1,), (1,)), ((), ())),
        preferred_element_type=jnp.float32,
    )
    scores = scores * factor + bias_ref[...]
    fresh_key = fresh_key * cosine_ref[...] + pltpu.roll(fresh_key, width // 2, 1) * sine_ref[...]
    fresh_key = fresh_key.astype(jnp.bfloat16).astype(jnp.float32)
    new_score = jnp.sum(query * fresh_key, axis=-1, keepdims=True) * factor
    peak = jnp.maximum(jnp.max(scores, axis=-1, keepdims=True), new_score)
    weights = jnp.exp(scores - peak)
    new_weight = jnp.exp(new_score - peak)
    totals = jnp.sum(weights, axis=-1, keepdims=True) + new_weight
    weights = pltpu.roll(weights, span, 1).astype(jnp.bfloat16)
    mixture = jnp.dot(weights, entries, preferred_element_type=jnp.float32)
    mixture = mixture + new_weight * fresh_value
    out_ref[...] = (mixture / totals).astype(jnp.bfloat16)


def add_product(attn_ref, weight_ref, resid_ref, out_ref):
    product = jnp.dot(attn_ref[...], weight_ref[...], preferred_element_type=jnp.float32)
    out_ref[...] = (resid_ref[...].astype(jnp.float32) + product).astype(out_ref.dtype)


def body(
    resid,
    norm_gain,
    query_weight,
    key_value_weight,
    out_weight,
    key_value_cache,
    lengths,
    positions,
):
    rows = resid.shape[1]
    devices = lax.axis_size(MINOR)
    groups = KEY_VALUE_HEADS
    members = devices // groups
    own_rows = rows // members
    me = lax.axis_index(MINOR)
    group, member = me // members, me % members
    span = key_value_cache.shape[2]

    pieces = key_value_cache[0].reshape(members, own_rows, span, 2, groups, HEAD_WIDTH)
    pieces = pieces.transpose(4, 0, 3, 2, 1, 5).reshape(
        devices, 2 * span, own_rows, HEAD_WIDTH
    )
    pieces = lax.optimization_barrier(jnp.pad(pieces, ((0, 0), (0, 1), (0, 0), (0, 0))))

    gathered = spread(resid[0])
    side, cores, line = gathered.shape[:3]
    cosine, sine = rotary_tables(positions[0])
    width = key_value_weight.shape[2]
    shares = HEAD_WIDTH // width
    whole, small = pl.BlockSpec(memory_space=pltpu.VMEM), pl.BlockSpec(memory_space=pltpu.SMEM)
    fresh, normed = pl.pallas_call(
        functools.partial(place_rows, cores, line),
        out_shape=(
            jax.ShapeDtypeStruct((rows, HEAD_WIDTH), jnp.bfloat16),
            jax.ShapeDtypeStruct((rows, query_weight.shape[1]), jnp.bfloat16),
        ),
        in_specs=[whole] * 3 + [small],
        out_specs=(whole, whole),
        compiler_params=pltpu.CompilerParams(vmem_limit_bytes=24 * 2**20),
    )(
        gathered.reshape((devices,) + resid.shape[1:]),
        norm_gain,
        key_value_weight[0].T,
        (me % shares).reshape(1),
    )
    query = pl.pallas_call(
        rotate_query,
        out_shape=jax.ShapeDtypeStruct((rows, HEAD_WIDTH), jnp.bfloat16),
        in_specs=[whole] * 4,
        out_specs=whole,
        compiler_params=pltpu.CompilerParams(vmem_limit_bytes=24 * 2**20),
    )(
        normed,
        query_weight[0],
        jnp.concatenate([cosine, cosine], axis=1),
        jnp.concatenate([-sine, sine], axis=1),
    )
    fresh = jnp.broadcast_to(fresh[None], (groups,) + fresh.shape)
    fresh = fresh.reshape(devices, 1, own_rows, HEAD_WIDTH)
    sent = lax.dynamic_update_slice_in_dim(pieces, fresh, pieces.shape[1] - 1, axis=1)
    arrived = lax.all_to_all(sent, MINOR, 0, 0).reshape(devices, -1, HEAD_WIDTH)
    chip = lax.all_gather(query, "c")
    chips = lax.axis_size("zb")
    near = [chip] + [
        lax.ppermute(chip, "zb", [(i, (i + by) % chips) for i in range(chips)])
        for by in range(1, chips)
    ]
    near = jnp.stack(near).reshape(members * rows, HEAD_WIDTH)
    per_device = arrived.shape[1]
    cached = 2 * span * own_rows
    entries = devices * per_device

    own_lengths = lax.dynamic_slice_in_dim(lengths[0], member * own_rows, own_rows)
    own_cosine = lax.dynamic_slice_in_dim(cosine, member * own_rows, own_rows)
    own_sine = lax.dynamic_slice_in_dim(sine, member * own_rows, own_rows)
    entry = jnp.arange(entries, dtype=jnp.int32)
    entry_from, entry_at = entry // per_device, entry % per_device
    entry_row = entry_at % own_rows
    entry_slot = entry_from * span + entry_at // own_rows
    rank = jnp.arange(members * own_rows, dtype=jnp.int32)[:, None]
    rank_row = rank % own_rows
    holders = [group * shares, devices // 2 + group * shares]
    select = jnp.concatenate(
        [
            (entry_at >= cached) & (entry_from // shares == holder // shares)
            & (entry_row == rank_row)
            for holder in holders
        ]
    ).astype(jnp.bfloat16)
    near_at = jnp.arange(members * rows, dtype=jnp.int32)
    per_chip = rows * members // chips
    near_chip = (lax.axis_index("zb") - near_at // per_chip) % chips
    near_from = near_chip * (members // chips) + near_at % per_chip // rows
    near_select = (near_from == rank // own_rows) & (
        near_at % rows == member * own_rows + rank_row
    )
    near_select = near_select.astype(jnp.bfloat16)
    live = (entry_at < span * own_rows) & (entry_row == rank_row)
    live = live & (entry_slot < jnp.tile(own_lengths, members)[:, None])
    bias = jnp.where(live, 0.0, -1e30)
    attn = pl.pallas_call(
        functools.partial(attend, span * own_rows, 1.0 / math.sqrt(HEAD_WIDTH)),
        out_shape=jax.ShapeDtypeStruct((members * own_rows, HEAD_WIDTH), jnp.bfloat16),
        in_specs=[whole] * 7,
        out_specs=whole,
        compiler_params=pltpu.CompilerParams(vmem_limit_bytes=24 * 2**20),
    )(
        arrived.reshape(entries, HEAD_WIDTH),
        near,
        select,
        near_select,
        bias,
        jnp.tile(jnp.concatenate([own_cosine, own_cosine], axis=1), (members, 1)),
        jnp.tile(jnp.concatenate([-own_sine, own_sine], axis=1), (members, 1)),
    )

    full = spread(attn)
    x, c, line = full.shape[:3]
    inner = members // c
    full = full.reshape(x, c, line // inner, inner, members, own_rows, HEAD_WIDTH)
    full = full.transpose(3, 1, 5, 0, 2, 4, 6).reshape(rows, -1)
    updated = pl.pallas_call(
        add_product,
        out_shape=jax.ShapeDtypeStruct(resid.shape[1:], resid.dtype),
        in_specs=[whole] * 3,
        out_specs=whole,
        compiler_params=pltpu.CompilerParams(vmem_limit_bytes=24 * 2**20),
    )(full, out_weight[0], resid[0])
    sections = lax.axis_size("section")
    following = [(i, (i + 1) % sections) for i in range(sections)]
    return lax.ppermute(updated, "section", following)[None]


def solution(mesh):
    sections, devices = mesh.devices.shape
    near = devices // KEY_VALUE_HEADS // 2
    split = Mesh(
        mesh.devices.reshape(sections, 2, devices // (4 * near), near, 2), ("section",) + MINOR
    )
    return jax.shard_map(
        body,
        mesh=split,
        in_specs=(
            P("section", None, MINOR),
            P("section", None),
            P("section", None, MINOR),
            P("section", None, MINOR),
            P("section", None, MINOR),
            P("section", None, MINOR, None),
            P("section", None),
            P("section", None),
        ),
        out_specs=P("section", None, MINOR),
        check_vma=False,
    )
```

```python
import functools
import math

import jax
import jax.numpy as jnp
from jax import lax
from jax.experimental import pallas as pl
from jax.experimental.pallas import tpu as pltpu
from jax.sharding import Mesh
from jax.sharding import PartitionSpec as P

HEAD_WIDTH = 128
KEY_VALUE_HEADS = 8
LINE = ("za", "zb")
MINOR = ("x",) + LINE + ("c",)


def rotary_tables(token_positions):
    half_size = HEAD_WIDTH // 2
    freqs = jnp.exp(
        -math.log(500000.0) * 2.0 * jnp.arange(half_size, dtype=jnp.float32) / HEAD_WIDTH
    )
    angles = token_positions.astype(jnp.float32)[:, None] * freqs
    return jnp.cos(angles), jnp.sin(angles)


def spread(part):
    line = lax.axis_size(LINE)
    copies = jnp.broadcast_to(part[None], (line,) + part.shape)
    along = lax.all_to_all(copies, LINE, 0, 0)
    full = lax.all_gather(along, ("x", "c"))
    return full.reshape((lax.axis_size("x"), lax.axis_size("c"), line) + part.shape)


def place_rows(cores, line, gathered_ref, gain_ref, keyval_ref, share_ref, fresh_ref, normed_ref):
    rows, width = gathered_ref.shape[1:]
    squares = jnp.zeros((rows, width), jnp.float32)
    for at in range(gathered_ref.shape[0]):
        wide = gathered_ref[at].astype(jnp.float32)
        squares = squares + wide * wide
    meansq = jnp.sum(squares, axis=-1, keepdims=True) / (gathered_ref.shape[0] * width)
    scale = lax.rsqrt(meansq + 1e-05)
    for at in range(gathered_ref.shape[0]):
        side, core, chip = at // (cores * line), at // line % cores, at % line
        first = ((side * line + chip) * cores + core) * width
        gain = gain_ref[:, first : first + width].astype(jnp.float32)
        wide = gathered_ref[at].astype(jnp.float32)
        normed_ref[:, first : first + width] = (wide * scale * gain).astype(jnp.bfloat16)
    keyval = lax.dot_general(
        normed_ref[...],
        keyval_ref[...],
        (((1,), (1,)), ((), ())),
        preferred_element_type=jnp.float32,
    ).astype(jnp.bfloat16)
    part = keyval.shape[1]
    shares = width // part
    wide = jnp.concatenate([keyval.astype(jnp.float32)] * shares, axis=1)
    lane = lax.broadcasted_iota(jnp.int32, (rows, width), 1)
    first = share_ref[0] * part
    kept = (lane >= first) & (lane < first + part)
    fresh_ref[...] = jnp.where(kept, wide, 0.0).astype(jnp.bfloat16)


def rotate_query(normed_ref, query_ref, cosine_ref, sine_ref, out_ref):
    query = jnp.dot(normed_ref[...], query_ref[...], preferred_element_type=jnp.float32)
    turned = pltpu.roll(query, query.shape[1] // 2, 1)
    query = query * cosine_ref[...] + turned * sine_ref[...]
    out_ref[...] = query.astype(jnp.bfloat16)


def attend(span, factor, entries_ref, near_ref, select_ref, near_select_ref, bias_ref, cosine_ref,
           sine_ref, out_ref):
    entries = entries_ref[...]
    rows, width = out_ref.shape
    picked = jnp.dot(select_ref[...], entries, preferred_element_type=jnp.float32)
    query = jnp.dot(near_select_ref[...], near_ref[...], preferred_element_type=jnp.float32)
    fresh_key, fresh_value = picked[:rows], picked[rows:]
    scores = lax.dot_general(
        query.astype(jnp.bfloat16),
        entries,
        (((1,), (1,)), ((), ())),
        preferred_element_type=jnp.float32,
    )
    scores = scores * factor + bias_ref[...]
    fresh_key = fresh_key * cosine_ref[...] + pltpu.roll(fresh_key, width // 2, 1) * sine_ref[...]
    fresh_key = fresh_key.astype(jnp.bfloat16).astype(jnp.float32)
    new_score = jnp.sum(query * fresh_key, axis=-1, keepdims=True) * factor
    peak = jnp.maximum(jnp.max(scores, axis=-1, keepdims=True), new_score)
    weights = jnp.exp(scores - peak)
    new_weight = jnp.exp(new_score - peak)
    totals = jnp.sum(weights, axis=-1, keepdims=True) + new_weight
    weights = pltpu.roll(weights, span, 1).astype(jnp.bfloat16)
    mixture = jnp.dot(weights, entries, preferred_element_type=jnp.float32)
    mixture = mixture + new_weight * fresh_value
    out_ref[...] = (mixture / totals).astype(jnp.bfloat16)


def add_product(attn_ref, weight_ref, resid_ref, out_ref):
    product = jnp.dot(attn_ref[...], weight_ref[...], preferred_element_type=jnp.float32)
    out_ref[...] = (resid_ref[...].astype(jnp.float32) + product).astype(out_ref.dtype)


def body(
    resid,
    norm_gain,
    query_weight,
    key_value_weight,
    out_weight,
    key_value_cache,
    lengths,
    positions,
):
    rows = resid.shape[1]
    devices = lax.axis_size(MINOR)
    groups = KEY_VALUE_HEADS
    members = devices // groups
    own_rows = rows // members
    me = lax.axis_index(MINOR)
    group, member = me // members, me % members
    span = key_value_cache.shape[2]

    pieces = key_value_cache[0].reshape(members, own_rows, span, 2, groups, HEAD_WIDTH)
    pieces = pieces.transpose(4, 0, 3, 2, 1, 5).reshape(
        devices, 2 * span, own_rows, HEAD_WIDTH
    )
    pieces = lax.optimization_barrier(jnp.pad(pieces, ((0, 0), (0, 1), (0, 0), (0, 0))))

    gathered = spread(resid[0])
    side, cores, line = gathered.shape[:3]
    cosine, sine = rotary_tables(positions[0])
    width = key_value_weight.shape[2]
    shares = HEAD_WIDTH // width
    whole, small = pl.BlockSpec(memory_space=pltpu.VMEM), pl.BlockSpec(memory_space=pltpu.SMEM)
    fresh, normed = pl.pallas_call(
        functools.partial(place_rows, cores, line),
        out_shape=(
            jax.ShapeDtypeStruct((rows, HEAD_WIDTH), jnp.bfloat16),
            jax.ShapeDtypeStruct((rows, query_weight.shape[1]), jnp.bfloat16),
        ),
        in_specs=[whole] * 3 + [small],
        out_specs=(whole, whole),
        compiler_params=pltpu.CompilerParams(vmem_limit_bytes=24 * 2**20),
    )(
        gathered.reshape((devices,) + resid.shape[1:]),
        norm_gain,
        key_value_weight[0].T,
        (me % shares).reshape(1),
    )
    query = pl.pallas_call(
        rotate_query,
        out_shape=jax.ShapeDtypeStruct((rows, HEAD_WIDTH), jnp.bfloat16),
        in_specs=[whole] * 4,
        out_specs=whole,
        compiler_params=pltpu.CompilerParams(vmem_limit_bytes=24 * 2**20),
    )(
        normed,
        query_weight[0],
        jnp.concatenate([cosine, cosine], axis=1),
        jnp.concatenate([-sine, sine], axis=1),
    )
    fresh = jnp.broadcast_to(fresh[None], (groups,) + fresh.shape)
    fresh = fresh.reshape(devices, 1, own_rows, HEAD_WIDTH)
    sent = lax.dynamic_update_slice_in_dim(pieces, fresh, pieces.shape[1] - 1, axis=1)
    arrived = lax.all_to_all(sent, MINOR, 0, 0).reshape(devices, -1, HEAD_WIDTH)
    chip = lax.all_gather(query, "c")
    chips = lax.axis_size("zb")
    near = [chip] + [
        lax.ppermute(chip, "zb", [(i, (i + by) % chips) for i in range(chips)])
        for by in range(1, chips)
    ]
    near = jnp.stack(near).reshape(members * rows, HEAD_WIDTH)
    per_device = arrived.shape[1]
    cached = 2 * span * own_rows
    entries = devices * per_device

    own_lengths = lax.dynamic_slice_in_dim(lengths[0], member * own_rows, own_rows)
    own_cosine = lax.dynamic_slice_in_dim(cosine, member * own_rows, own_rows)
    own_sine = lax.dynamic_slice_in_dim(sine, member * own_rows, own_rows)
    entry = jnp.arange(entries, dtype=jnp.int32)
    entry_from, entry_at = entry // per_device, entry % per_device
    entry_row = entry_at % own_rows
    entry_slot = entry_from * span + entry_at // own_rows
    rank = jnp.arange(members * own_rows, dtype=jnp.int32)[:, None]
    rank_row = rank % own_rows
    holders = [group * shares, devices // 2 + group * shares]
    select = jnp.concatenate(
        [
            (entry_at >= cached) & (entry_from // shares == holder // shares)
            & (entry_row == rank_row)
            for holder in holders
        ]
    ).astype(jnp.bfloat16)
    near_at = jnp.arange(members * rows, dtype=jnp.int32)
    per_chip = rows * members // chips
    near_chip = (lax.axis_index("zb") - near_at // per_chip) % chips
    near_from = near_chip * (members // chips) + near_at % per_chip // rows
    near_select = (near_from == rank // own_rows) & (
        near_at % rows == member * own_rows + rank_row
    )
    near_select = near_select.astype(jnp.bfloat16)
    live = (entry_at < span * own_rows) & (entry_row == rank_row)
    live = live & (entry_slot < jnp.tile(own_lengths, members)[:, None])
    bias = jnp.where(live, 0.0, -1e30)
    attn = pl.pallas_call(
        functools.partial(attend, span * own_rows, 1.0 / math.sqrt(HEAD_WIDTH)),
        out_shape=jax.ShapeDtypeStruct((members * own_rows, HEAD_WIDTH), jnp.bfloat16),
        in_specs=[whole] * 7,
        out_specs=whole,
        compiler_params=pltpu.CompilerParams(vmem_limit_bytes=24 * 2**20),
    )(
        arrived.reshape(entries, HEAD_WIDTH),
        near,
        select,
        near_select,
        bias,
        jnp.tile(jnp.concatenate([own_cosine, own_cosine], axis=1), (members, 1)),
        jnp.tile(jnp.concatenate([-own_sine, own_sine], axis=1), (members, 1)),
    )

    full = spread(attn)
    x, c, line = full.shape[:3]
    inner = members // c
    full = full.reshape(x, c, line // inner, inner, members, own_rows, HEAD_WIDTH)
    full = full.transpose(3, 1, 5, 0, 2, 4, 6).reshape(rows, -1)
    updated = pl.pallas_call(
        add_product,
        out_shape=jax.ShapeDtypeStruct(resid.shape[1:], resid.dtype),
        in_specs=[whole] * 3,
        out_specs=whole,
        compiler_params=pltpu.CompilerParams(vmem_limit_bytes=24 * 2**20),
    )(full, out_weight[0], resid[0])
    sections = lax.axis_size("section")
    following = [(i, (i + 1) % sections) for i in range(sections)]
    return lax.ppermute(updated, "section", following)[None]


def solution(mesh):
    sections, devices = mesh.devices.shape
    near = devices // KEY_VALUE_HEADS // 2
    split = Mesh(
        mesh.devices.reshape(sections, 2, devices // (4 * near), near, 2), ("section",) + MINOR
    )
    return jax.shard_map(
        body,
        mesh=split,
        in_specs=(
            P("section", None, MINOR),
            P("section", None),
            P("section", None, MINOR),
            P("section", None, MINOR),
            P("section", None, MINOR),
            P("section", None, MINOR, None),
            P("section", None),
            P("section", None),
        ),
        out_specs=P("section", None, MINOR),
        check_vma=False,
    )
```

```python
import functools
import math

import jax
import jax.numpy as jnp
from jax import lax
from jax.experimental import pallas as pl
from jax.experimental.pallas import tpu as pltpu
from jax.sharding import Mesh
from jax.sharding import PartitionSpec as P

HEAD_WIDTH = 128
KEY_VALUE_HEADS = 8
LINE = ("za", "zb")
MINOR = ("x",) + LINE + ("c",)


def rotary_tables(token_positions):
    half_size = HEAD_WIDTH // 2
    freqs = jnp.exp(
        -math.log(500000.0) * 2.0 * jnp.arange(half_size, dtype=jnp.float32) / HEAD_WIDTH
    )
    angles = token_positions.astype(jnp.float32)[:, None] * freqs
    return jnp.cos(angles), jnp.sin(angles)


def spread(part):
    line = lax.axis_size(LINE)
    copies = jnp.broadcast_to(part[None], (line,) + part.shape)
    along = lax.all_to_all(copies, LINE, 0, 0)
    full = lax.all_gather(along, ("x", "c"))
    return full.reshape((lax.axis_size("x"), lax.axis_size("c"), line) + part.shape)


def place_rows(cores, line, gathered_ref, gain_ref, keyval_ref, share_ref, fresh_ref, normed_ref):
    rows, width = gathered_ref.shape[1:]
    squares = jnp.zeros((rows, width), jnp.float32)
    for at in range(gathered_ref.shape[0]):
        wide = gathered_ref[at].astype(jnp.float32)
        squares = squares + wide * wide
    meansq = jnp.sum(squares, axis=-1, keepdims=True) / (gathered_ref.shape[0] * width)
    scale = lax.rsqrt(meansq + 1e-05)
    for at in range(gathered_ref.shape[0]):
        side, core, chip = at // (cores * line), at // line % cores, at % line
        first = ((side * line + chip) * cores + core) * width
        gain = gain_ref[:, first : first + width].astype(jnp.float32)
        wide = gathered_ref[at].astype(jnp.float32)
        normed_ref[:, first : first + width] = (wide * scale * gain).astype(jnp.bfloat16)
    keyval = lax.dot_general(
        normed_ref[...],
        keyval_ref[...],
        (((1,), (1,)), ((), ())),
        preferred_element_type=jnp.float32,
    ).astype(jnp.bfloat16)
    part = keyval.shape[1]
    lane = lax.broadcasted_iota(jnp.int32, (part, width), 1)
    column = lax.broadcasted_iota(jnp.int32, (part, width), 0)
    place = jnp.where(lane == column + share_ref[0] * part, 1.0, 0.0).astype(jnp.bfloat16)
    placed = jnp.dot(keyval, place, preferred_element_type=jnp.float32)
    fresh_ref[...] = placed.astype(jnp.bfloat16)


def rotate_query(normed_ref, query_ref, cosine_ref, sine_ref, out_ref):
    query = jnp.dot(normed_ref[...], query_ref[...], preferred_element_type=jnp.float32)
    turned = pltpu.roll(query, query.shape[1] // 2, 1)
    query = query * cosine_ref[...] + turned * sine_ref[...]
    out_ref[...] = query.astype(jnp.bfloat16)


def attend(span, factor, entries_ref, near_ref, select_ref, near_select_ref, bias_ref, cosine_ref,
           sine_ref, out_ref):
    entries = entries_ref[...]
    rows, width = out_ref.shape
    picked = jnp.dot(select_ref[...], entries, preferred_element_type=jnp.float32)
    query = jnp.dot(near_select_ref[...], near_ref[...], preferred_element_type=jnp.float32)
    fresh_key, fresh_value = picked[:rows], picked[rows:]
    scores = lax.dot_general(
        query.astype(jnp.bfloat16),
        entries,
        (((1,), (1,)), ((), ())),
        preferred_element_type=jnp.float32,
    )
    scores = scores * factor + bias_ref[...]
    fresh_key = fresh_key * cosine_ref[...] + pltpu.roll(fresh_key, width // 2, 1) * sine_ref[...]
    fresh_key = fresh_key.astype(jnp.bfloat16).astype(jnp.float32)
    new_score = jnp.sum(query * fresh_key, axis=-1, keepdims=True) * factor
    peak = jnp.maximum(jnp.max(scores, axis=-1, keepdims=True), new_score)
    weights = jnp.exp(scores - peak)
    new_weight = jnp.exp(new_score - peak)
    totals = jnp.sum(weights, axis=-1, keepdims=True) + new_weight
    weights = pltpu.roll(weights.astype(jnp.bfloat16), span, 1)
    mixture = jnp.dot(weights, entries, preferred_element_type=jnp.float32)
    mixture = mixture + new_weight * fresh_value
    out_ref[...] = (mixture / totals).astype(jnp.bfloat16)


def add_product(attn_ref, weight_ref, resid_ref, out_ref):
    product = jnp.dot(attn_ref[...], weight_ref[...], preferred_element_type=jnp.float32)
    out_ref[...] = (resid_ref[...].astype(jnp.float32) + product).astype(out_ref.dtype)


def body(
    resid,
    norm_gain,
    query_weight,
    key_value_weight,
    out_weight,
    key_value_cache,
    lengths,
    positions,
):
    rows = resid.shape[1]
    devices = lax.axis_size(MINOR)
    groups = KEY_VALUE_HEADS
    members = devices // groups
    own_rows = rows // members
    me = lax.axis_index(MINOR)
    group, member = me // members, me % members
    span = key_value_cache.shape[2]

    pieces = key_value_cache[0].reshape(members, own_rows, span, 2, groups, HEAD_WIDTH)
    pieces = pieces.transpose(4, 0, 3, 2, 1, 5).reshape(
        devices, 2 * span, own_rows, HEAD_WIDTH
    )
    pieces = lax.optimization_barrier(jnp.pad(pieces, ((0, 0), (0, 1), (0, 0), (0, 0))))

    gathered = spread(resid[0])
    side, cores, line = gathered.shape[:3]
    cosine, sine = rotary_tables(positions[0])
    width = key_value_weight.shape[2]
    shares = HEAD_WIDTH // width
    whole, small = pl.BlockSpec(memory_space=pltpu.VMEM), pl.BlockSpec(memory_space=pltpu.SMEM)
    fresh, normed = pl.pallas_call(
        functools.partial(place_rows, cores, line),
        out_shape=(
            jax.ShapeDtypeStruct((rows, HEAD_WIDTH), jnp.bfloat16),
            jax.ShapeDtypeStruct((rows, query_weight.shape[1]), jnp.bfloat16),
        ),
        in_specs=[whole] * 3 + [small],
        out_specs=(whole, whole),
        compiler_params=pltpu.CompilerParams(vmem_limit_bytes=24 * 2**20),
    )(
        gathered.reshape((devices,) + resid.shape[1:]),
        norm_gain,
        key_value_weight[0].T,
        (me % shares).reshape(1),
    )
    query = pl.pallas_call(
        rotate_query,
        out_shape=jax.ShapeDtypeStruct((rows, HEAD_WIDTH), jnp.bfloat16),
        in_specs=[whole] * 4,
        out_specs=whole,
        compiler_params=pltpu.CompilerParams(vmem_limit_bytes=24 * 2**20),
    )(
        normed,
        query_weight[0],
        jnp.concatenate([cosine, cosine], axis=1),
        jnp.concatenate([-sine, sine], axis=1),
    )
    fresh = jnp.broadcast_to(fresh[None], (groups,) + fresh.shape)
    fresh = fresh.reshape(devices, 1, own_rows, HEAD_WIDTH)
    sent = lax.dynamic_update_slice_in_dim(pieces, fresh, pieces.shape[1] - 1, axis=1)
    arrived = lax.all_to_all(sent, MINOR, 0, 0).reshape(devices, -1, HEAD_WIDTH)
    chip = lax.all_gather(query, "c")
    chips = lax.axis_size("zb")
    near = [chip] + [
        lax.ppermute(chip, "zb", [(i, (i + by) % chips) for i in range(chips)])
        for by in range(1, chips)
    ]
    near = jnp.stack(near).reshape(members * rows, HEAD_WIDTH)
    per_device = arrived.shape[1]
    cached = 2 * span * own_rows
    entries = devices * per_device

    own_lengths = lax.dynamic_slice_in_dim(lengths[0], member * own_rows, own_rows)
    own_cosine = lax.dynamic_slice_in_dim(cosine, member * own_rows, own_rows)
    own_sine = lax.dynamic_slice_in_dim(sine, member * own_rows, own_rows)
    entry = jnp.arange(entries, dtype=jnp.int32)
    entry_from, entry_at = entry // per_device, entry % per_device
    entry_row = entry_at % own_rows
    entry_slot = entry_from * span + entry_at // own_rows
    rank = jnp.arange(members * own_rows, dtype=jnp.int32)[:, None]
    rank_row = rank % own_rows
    holders = [group * shares, devices // 2 + group * shares]
    select = jnp.concatenate(
        [
            (entry_at >= cached) & (entry_from // shares == holder // shares)
            & (entry_row == rank_row)
            for holder in holders
        ]
    ).astype(jnp.bfloat16)
    near_at = jnp.arange(members * rows, dtype=jnp.int32)
    per_chip = rows * members // chips
    near_chip = (lax.axis_index("zb") - near_at // per_chip) % chips
    near_from = near_chip * (members // chips) + near_at % per_chip // rows
    near_select = (near_from == rank // own_rows) & (
        near_at % rows == member * own_rows + rank_row
    )
    near_select = near_select.astype(jnp.bfloat16)
    live = (entry_at < span * own_rows) & (entry_row == rank_row)
    live = live & (entry_slot < jnp.tile(own_lengths, members)[:, None])
    bias = jnp.where(live, 0.0, -1e30)
    attn = pl.pallas_call(
        functools.partial(attend, span * own_rows, 1.0 / math.sqrt(HEAD_WIDTH)),
        out_shape=jax.ShapeDtypeStruct((members * own_rows, HEAD_WIDTH), jnp.bfloat16),
        in_specs=[whole] * 7,
        out_specs=whole,
        compiler_params=pltpu.CompilerParams(vmem_limit_bytes=24 * 2**20),
    )(
        arrived.reshape(entries, HEAD_WIDTH),
        near,
        select,
        near_select,
        bias,
        jnp.tile(jnp.concatenate([own_cosine, own_cosine], axis=1), (members, 1)),
        jnp.tile(jnp.concatenate([-own_sine, own_sine], axis=1), (members, 1)),
    )

    full = spread(attn)
    x, c, line = full.shape[:3]
    inner = members // c
    full = full.reshape(x, c, line // inner, inner, members, own_rows, HEAD_WIDTH)
    full = full.transpose(3, 1, 5, 0, 2, 4, 6).reshape(rows, -1)
    updated = pl.pallas_call(
        add_product,
        out_shape=jax.ShapeDtypeStruct(resid.shape[1:], resid.dtype),
        in_specs=[whole] * 3,
        out_specs=whole,
        compiler_params=pltpu.CompilerParams(vmem_limit_bytes=24 * 2**20),
    )(full, out_weight[0], resid[0])
    sections = lax.axis_size("section")
    following = [(i, (i + 1) % sections) for i in range(sections)]
    return lax.ppermute(updated, "section", following)[None]


def solution(mesh):
    sections, devices = mesh.devices.shape
    near = devices // KEY_VALUE_HEADS // 2
    split = Mesh(
        mesh.devices.reshape(sections, 2, devices // (4 * near), near, 2), ("section",) + MINOR
    )
    return jax.shard_map(
        body,
        mesh=split,
        in_specs=(
            P("section", None, MINOR),
            P("section", None),
            P("section", None, MINOR),
            P("section", None, MINOR),
            P("section", None, MINOR),
            P("section", None, MINOR, None),
            P("section", None),
            P("section", None),
        ),
        out_specs=P("section", None, MINOR),
        check_vma=False,
    )
```
